256 devices in a mesh: row: 16 (over y, x), col: 16 (over z, core).
Axes of the slice: x: 4, y: 4, z: 8, core: 2. Of those that a mesh axis runs over, the one named last changes fastest.
Arguments:
- a_vals: float32 [128, 64, 128, 128], P('row', 'col'), may hold values from -0.109375 to 0.109375
- a_cols: int32 [128, 64], P('row', 'col'), may hold values from 0 to 127, as said below
- a_count: int32 [128, 16], P('row', 'col'), may hold values from 0 to 4, as said below
- p_vals: float32 [128, 8, 128, 128], P('row'), may hold values from -0.75 to 0.75
- p_cols: int32 [128, 8], replicated, may hold values from 0 to 15, as said below
Outputs:
- c_out: float32 [16, 16, 128, 128], P('row', 'col')
The draws below stay inside these ranges and needn't reach their ends.
Inputs may be any that keep to these rules, and one draw needn't show every extreme that they name: `a_cols`: the entry in slot column s lies in the fine tile columns of grid column s // 4, from (s // 4) * 8 to (s // 4 + 1) * 8 - 1. With h = i // 8: a_count[i, c] is 4 for c = h and for c = (h + 8) mod 16; between 1 and 4 for other c within cyclic distance 2 of h; 0 for all other c. With h = i // 8: p_cols[i, 0] = h, p_cols[i, 1] = (h + 8) mod 16, and every other p_cols[i, t] lies within cyclic distance 2 of h.
All inputs are finite; a program needn't handle non-finite values.
Results may differ from the reference program's by a relative error of at most 0.0003.
Values sent between devices are 32-bit elements; how exact they have to be, the bound alone decides.
A program may use at most 128 MiB of HBM per device.

```python
import jax
import jax.numpy as jnp
from jax import lax

B = 128
TPC = 8
KS = 4
KP = 8
NF = 128
NC = 16
N_COL = 16


def draw_a_cols(key, part):
    key = jax.random.fold_in(key, 11)
    cell_count = NF // TPC
    offsets = jax.random.randint(key, (NF, KS * cell_count), 0, TPC, dtype=jnp.int32)
    cell_ids = jnp.arange(KS * cell_count, dtype=jnp.int32) // KS
    return (offsets + cell_ids[None, :] * TPC).astype(jnp.int32)


def draw_a_count(key, part):
    key = jax.random.fold_in(key, 13)
    counts = jax.random.randint(key, (NF, NC), 1, KS + 1, dtype=jnp.int32)
    home = jnp.arange(NF, dtype=jnp.int32) // TPC
    cells = jnp.arange(NC, dtype=jnp.int32)
    apart = (cells[None, :] - home[:, None]) % NC
    reach = jnp.minimum(apart, NC - apart)
    counts = jnp.where(reach <= 2, counts, 0)
    counts = jnp.where(reach == 0, KS, counts)
    counts = jnp.where(apart == NC // 2, KS, counts)
    return counts.astype(jnp.int32)


def draw_p_cols(key, part):
    key = jax.random.fold_in(key, 17)
    offsets = jax.random.randint(key, (NF, KP), -2, 3, dtype=jnp.int32)
    offsets = offsets.at[:, 0].set(0)
    offsets = offsets.at[:, 1].set(NC // 2)
    home = jnp.arange(NF, dtype=jnp.int32) // TPC
    return ((home[:, None] + offsets) % NC).astype(jnp.int32)


def block_levels(own_key, extent, cuts, low, largest):
    def one(axis_at, blocks):
        draws = jax.random.uniform(jax.random.fold_in(jax.random.fold_in(own_key, 6), axis_at), (blocks,), jnp.float32, low / len(cuts), largest / len(cuts))
        return jnp.repeat(jnp.exp(draws), extent[axis_at] // blocks).reshape((-1,) + (1,) * (len(extent) - axis_at - 1))

    factor_of = one(*cuts[0])
    for cut in cuts[1:]:
        factor_of = factor_of * one(*cut)
    return factor_of


def scatter_about(stream_key, shape, spread, most, cuts=(), kind=jnp.bfloat16):
    drawn = spread * jax.random.normal(stream_key, shape, jnp.float32)
    if cuts:
        drawn = drawn * block_levels(stream_key, shape, cuts, -0.22, 0.18)
    return jnp.clip(drawn, -most, most).astype(kind)


def setup_inputs(seed: int = 0) -> dict:
    splits = jax.random.split(jax.random.key(seed), 6)
    a_vals = scatter_about(splits[0], (NF, KS * N_COL, B, B), (B * KS * 6) ** -0.5, 0.109375, ((0, 16), (1, 16)), jnp.float32)
    a_cols = draw_a_cols(jax.random.fold_in(splits[5], 71), 0)
    a_count = draw_a_count(jax.random.fold_in(splits[5], 71), 0)
    p_vals = scatter_about(splits[3], (NF, KP, B, B), (B // 2) ** -0.5, 0.75, ((0, 16),), jnp.float32)
    p_cols = draw_p_cols(jax.random.fold_in(splits[5], 71), 0)
    return {"a_vals": a_vals, "a_cols": a_cols, "a_count": a_count, "p_vals": p_vals, "p_cols": p_cols}


highest = lax.Precision.HIGHEST


def reference(a_vals, a_cols, a_count, p_vals, p_cols):
    slot_total = a_cols.shape[1]
    slot_ids = jnp.arange(slot_total, dtype=jnp.int32)
    coarse_ids = jnp.arange(NC, dtype=jnp.int32)

    def product_row(row_args):
        a_tiles, col_ids, live_count = row_args
        live_mask = ((slot_ids % KS) < jnp.repeat(live_count, KS)).astype(jnp.float32)
        gathered = p_vals[col_ids]
        products = jnp.einsum('sab,stbc->stac', a_tiles * live_mask[:, None, None], gathered, precision=highest)
        placing = (p_cols[col_ids][:, :, None] == coarse_ids[None, None, :]).astype(jnp.float32)
        return jnp.einsum('stJ,stac->Jac', placing, products, precision=highest)

    ap_whole = lax.map(product_row, (a_vals, a_cols, a_count))

    def restrict(running, row_args):
        p_tiles, col_ids, row_ap = row_args
        placing = (col_ids[:, None] == coarse_ids[None, :]).astype(jnp.float32)
        weighted = jnp.einsum('tba,Jbc->tJac', p_tiles, row_ap, precision=highest)
        return running + jnp.einsum('tI,tJac->IJac', placing, weighted, precision=highest), None

    c_out, scan_tail = lax.scan(restrict, jnp.zeros((NC, NC, B, B), jnp.float32), (p_vals, p_cols, ap_whole))
    return c_out
```

```python
import jax
import jax.numpy as jnp
from jax import lax
from jax.experimental import pallas as pl
from jax.experimental.pallas import tpu as pltpu
from jax.sharding import PartitionSpec as P

MESH = pl.DeviceIdType.MESH
N = 16
REACH = (8, 2, 14, 1, 15, 0)
PLACE = {0: 0, 1: 15, 2: 2, 3: 13, 4: 9, 6: 5, 7: 4, 8: 8, 9: 12, 10: 11, 12: 7, 13: 3, 14: 14, 15: 1}
ROWS = 8
SLOTS = 4
B = 128
K = ROWS * B


def pick(table, index):
    total = jnp.int32(0)
    for key, value in table.items():
        total = jnp.where(index == key, jnp.int32(value), total)
    return total


def among(keys, index):
    hit = index == keys[0]
    for key in keys[1:]:
        hit = jnp.logical_or(hit, index == key)
    return hit


def split(x):
    high = x.astype(jnp.bfloat16)
    return high, (x - high.astype(jnp.float32)).astype(jnp.bfloat16)


def dot3(left_high, left_low, right_high, right_low):
    total = jnp.dot(left_high, right_high, preferred_element_type=jnp.float32)
    total += jnp.dot(left_high, right_low, preferred_element_type=jnp.float32)
    return total + jnp.dot(left_low, right_high, preferred_element_type=jnp.float32)


JOBS = {place: job for job, place in PLACE.items()}
REACH_AT = {offset: at for at, offset in enumerate(REACH)}


def kernel(
    a_cols, a_count, p_cols, a_hbm, p_hbm, out,
    a_ref, p_ref, a_high, a_low, p_high, p_low, t_high, t_low,
    q_send, q_recv, c_send, c_recv, total,
    load_sem, q_send_sem, q_recv_sem, c_send_sem, c_recv_sem,
):
    row, col = lax.axis_index("row"), lax.axis_index("col")
    mine = lax.rem(col - row + N, N)
    live = among(REACH, mine)
    has_job = among(tuple(JOBS), mine)
    job = pick(JOBS, mine)
    coarse = lax.rem(row + job, N)

    load_a = pltpu.make_async_copy(a_hbm, a_ref, load_sem.at[0])
    load_p = pltpu.make_async_copy(p_hbm, p_ref, load_sem.at[1])
    load_a.start()
    load_p.start()

    def q_copy(at):
        offset = lax.rem(REACH[at] - mine + N, N)
        place = pick(PLACE, offset)
        slot = pick(REACH_AT, mine)
        target = lax.rem(col + place, N)
        own = jnp.logical_and(mine == 0, place == 0)
        copy = pltpu.make_async_remote_copy(
            src_ref=q_send.at[at], dst_ref=q_recv.at[slot],
            send_sem=q_send_sem.at[at], recv_sem=q_recv_sem.at[slot],
            device_id=(col, target), device_id_type=MESH,
        )
        return copy, own

    def q_source(at):
        used = jnp.logical_and(has_job, among(REACH, lax.rem(job + REACH[at], N)))
        source = lax.rem(row - REACH[at] + N, N)
        own = source == row if REACH[at] == 0 else jnp.bool_(False)
        own = jnp.logical_and(own, mine == 0)
        return used, own, source

    def c_copy(at):
        target = lax.rem(row + REACH[at], N)
        own = jnp.logical_and(coarse == row, target == col)
        copy = pltpu.make_async_remote_copy(
            src_ref=c_send.at[at], dst_ref=c_recv.at[at],
            send_sem=c_send_sem.at[at], recv_sem=c_recv_sem.at[at],
            device_id=(coarse, target), device_id_type=MESH,
        )
        return copy, own

    def c_source(at):
        fine = lax.rem(col - REACH[at] + N, N)
        offset = lax.rem(row - fine + N, N)
        used = among(tuple(PLACE), offset)
        place = lax.rem(fine + pick(PLACE, offset), N)
        own = jnp.logical_and(fine == row, place == col)
        return used, own, (fine, place)

    both = jnp.logical_and
    barrier = pltpu.get_barrier_semaphore()
    awaited = jnp.int32(0)
    for at in range(len(REACH)):
        used, own, source = q_source(at)

        @pl.when(both(used, ~own))
        def _():
            pl.semaphore_signal(barrier, inc=1, device_id=(source, row), device_id_type=MESH)

        used, own, source = c_source(at)

        @pl.when(both(used, ~own))
        def _():
            pl.semaphore_signal(barrier, inc=1, device_id=source, device_id_type=MESH)

        awaited += jnp.where(both(live, ~q_copy(at)[1]), 1, 0)
        awaited += jnp.where(both(has_job, ~c_copy(at)[1]), 1, 0)

    load_a.wait()

    @pl.when(live)
    def _():
        def build(i, carry):
            for k in range(ROWS):
                tile = jnp.zeros((B, B), jnp.float32)
                for s in range(SLOTS):
                    hit = jnp.logical_and(a_cols[i, s] == col * ROWS + k, s < a_count[i, 0])
                    tile += jnp.where(hit, 1.0, 0.0) * a_ref[i, s]
                high, low = split(tile)
                rows = pl.ds(pl.multiple_of(i * B, B), B)
                a_high[rows, k * B:(k + 1) * B] = high
                a_low[rows, k * B:(k + 1) * B] = low
            return carry

        lax.fori_loop(0, ROWS, build, 0)

    load_p.wait()

    @pl.when(awaited > 0)
    def _():
        pl.semaphore_wait(barrier, awaited)

    for at in range(len(REACH)):
        wanted = lax.rem(row + REACH[at], N)

        def merge(i, carry):
            tile = jnp.zeros((B, B), jnp.float32)
            for t in range(8):
                hit = p_cols[row * ROWS + i, t] == wanted
                tile += jnp.where(hit, 1.0, 0.0) * p_ref[i, t]
            rows = pl.ds(pl.multiple_of(i * B, B), B)
            high, low = split(tile)
            p_high[rows, at * B:(at + 1) * B] = high
            p_low[rows, at * B:(at + 1) * B] = low
            high, low = split(tile.T)
            t_high[:, rows] = high
            t_low[:, rows] = low
            return carry

        lax.fori_loop(0, ROWS, merge, 0)

        @pl.when(live)
        def _():
            def chunk(n, carry):
                cols = pl.ds(pl.multiple_of(n * 256, 256), 256)
                q_send[at, :, cols] = dot3(t_high[...], t_low[...], a_high[:, cols], a_low[:, cols])
                return carry

            lax.fori_loop(0, K // 256, chunk, 0)
            copy, own = q_copy(at)

            @pl.when(~own)
            def _():
                copy.start()

    @pl.when(has_job)
    def _():
        total[...] = jnp.zeros_like(total)
        for at in range(len(REACH)):
            used, own, _ = q_source(at)

            @pl.when(both(used, ~own))
            def _():
                pltpu.make_async_remote_copy(
                    src_ref=q_send.at[at], dst_ref=q_recv.at[at],
                    send_sem=q_send_sem.at[at], recv_sem=q_recv_sem.at[at],
                    device_id=(row, col), device_id_type=MESH,
                ).wait_recv()
                total[...] += q_recv[at]

            @pl.when(both(used, own))
            def _():
                total[...] += q_send[pick(REACH_AT, job)]

        high, low = split(total[...])
        for n in range(3):
            tiles = dot3(high, low, p_high[:, n * 256:(n + 1) * 256], p_low[:, n * 256:(n + 1) * 256])
            for half in range(2):
                at = 2 * n + half
                c_send[at] = tiles[:, half * B:(half + 1) * B]
                copy, own = c_copy(at)

                @pl.when(~own)
                def _():
                    copy.start()

    out[...] = jnp.zeros_like(out)
    for at in range(len(REACH)):
        used, own, _ = c_source(at)

        @pl.when(both(used, ~own))
        def _():
            pltpu.make_async_remote_copy(
                src_ref=c_send.at[at], dst_ref=c_recv.at[at],
                send_sem=c_send_sem.at[at], recv_sem=c_recv_sem.at[at],
                device_id=(row, col), device_id_type=MESH,
            ).wait_recv()
            out[0, 0] += c_recv[at]

        @pl.when(both(used, own))
        def _():
            out[0, 0] += c_send[at]

    for at in range(len(REACH)):
        copy, own = q_copy(at)

        @pl.when(both(live, ~own))
        def _():
            copy.wait_send()

        copy, own = c_copy(at)

        @pl.when(both(has_job, ~own))
        def _():
            copy.wait_send()


def on_device(a_vals, a_cols, a_count, p_vals, p_cols):
    smem = pl.BlockSpec(memory_space=pltpu.SMEM)
    hbm = pl.BlockSpec(memory_space=pl.ANY)
    spots = len(REACH)
    return pl.pallas_call(
        kernel,
        out_shape=jax.ShapeDtypeStruct((1, 1, B, B), jnp.float32),
        in_specs=[smem, smem, smem, hbm, hbm],
        out_specs=pl.BlockSpec(memory_space=pltpu.VMEM),
        scratch_shapes=[
            pltpu.VMEM((ROWS, SLOTS, B, B), jnp.float32),
            pltpu.VMEM((ROWS, 8, B, B), jnp.float32),
            pltpu.VMEM((K, K), jnp.bfloat16),
            pltpu.VMEM((K, K), jnp.bfloat16),
            pltpu.VMEM((K, spots * B), jnp.bfloat16),
            pltpu.VMEM((K, spots * B), jnp.bfloat16),
            pltpu.VMEM((B, K), jnp.bfloat16),
            pltpu.VMEM((B, K), jnp.bfloat16),
            pltpu.VMEM((spots, B, K), jnp.float32),
            pltpu.VMEM((spots, B, K), jnp.float32),
            pltpu.VMEM((spots, B, B), jnp.float32),
            pltpu.VMEM((spots, B, B), jnp.float32),
            pltpu.VMEM((B, K), jnp.float32),
            pltpu.SemaphoreType.DMA((2,)),
            pltpu.SemaphoreType.DMA((spots,)),
            pltpu.SemaphoreType.DMA((spots,)),
            pltpu.SemaphoreType.DMA((spots,)),
            pltpu.SemaphoreType.DMA((spots,)),
        ],
        compiler_params=pltpu.CompilerParams(
            collective_id=0, has_side_effects=True, vmem_limit_bytes=40 << 20
        ),
    )(a_cols, a_count, p_cols, a_vals, p_vals)


def solution(mesh):
    return jax.shard_map(
        on_device,
        mesh=mesh,
        in_specs=(
            P("row", "col", None, None),
            P("row", "col"),
            P("row", "col"),
            P("row", None, None, None),
            P(),
        ),
        out_specs=P("row", "col", None, None),
        check_vma=False,
    )
```

```python
import jax
import jax.numpy as jnp
from jax import lax
from jax.experimental import pallas as pl
from jax.experimental.pallas import tpu as pltpu
from jax.sharding import PartitionSpec as P

MESH = pl.DeviceIdType.MESH
N = 16
REACH = (8, 2, 14, 1, 15, 0)
PLACE = (
    {0: 5, 1: 60, 2: 4, 3: 0, 4: 32, 6: 8, 7: 25, 8: 56, 9: 52, 10: 44, 12: 24, 13: 9, 14: 1, 15: 61},
    {0: 1, 1: 4, 2: 61, 3: 56, 4: 36, 6: 28, 7: 24, 8: 8, 9: 52, 10: 40, 12: 16, 13: 60, 14: 0, 15: 5},
)
JOBS = 2
ROWS = 8
SLOTS = 4
B = 128
K = ROWS * B
PARTS = 4
CHUNK = 1024


def pick(table, index):
    total = jnp.int32(0)
    for key, value in table.items():
        total = jnp.where(index == key, jnp.int32(value), total)
    return total


def among(keys, index):
    hit = index == keys[0]
    for key in keys[1:]:
        hit = jnp.logical_or(hit, index == key)
    return hit


def split(x):
    high = x.astype(jnp.bfloat16)
    return high, (x - high.astype(jnp.float32)).astype(jnp.bfloat16)


def dot3(left_high, left_low, right_high, right_low):
    total = jnp.dot(left_high, right_high, preferred_element_type=jnp.float32)
    total += jnp.dot(left_high, right_low, preferred_element_type=jnp.float32)
    return total + jnp.dot(left_low, right_high, preferred_element_type=jnp.float32)


REACH_AT = {offset: at for at, offset in enumerate(REACH)}


def place_of(fine, offset):
    code = jnp.where(fine % 2 == 0, pick(PLACE[0], offset), pick(PLACE[1], offset))
    return code // 4, code % 4


def job_of(fine, place, slot):
    tables = [{code // 4: job + 1 for job, code in table.items() if code % 4 == slot} for table in PLACE]
    return jnp.where(fine % 2 == 0, pick(tables[0], place), pick(tables[1], place)) - 1


def kernel(
    a_cols, a_count, p_cols, a_hbm, p_hbm, out,
    a_ref, p_ref, a_high, a_low, p_high, p_low, sums,
    q_send, q_recv, c_send, c_recv, total,
    load_sem, q_send_sem, q_recv_sem, c_send_sem, c_recv_sem,
):
    row, col = lax.axis_index("row"), lax.axis_index("col")
    mine = lax.rem(col - row + N, N)
    live = among(REACH, mine)
    jobs = [job_of(row, mine, slot) for slot in range(JOBS)]

    load_a = pltpu.make_async_copy(a_hbm, a_ref, load_sem.at[0])
    load_p = pltpu.make_async_copy(p_hbm, p_ref, load_sem.at[1])
    load_a.start()
    load_p.start()

    def q_copy(at):
        offset = lax.rem(REACH[at] - mine + N, N)
        place, slot = place_of(col, offset)
        spot = pick(REACH_AT, mine)
        own = jnp.logical_and(mine == 0, place == 0)
        copy = pltpu.make_async_remote_copy(
            src_ref=q_send.at[at], dst_ref=q_recv.at[slot, spot],
            send_sem=q_send_sem.at[at], recv_sem=q_recv_sem.at[slot, spot],
            device_id=(col, lax.rem(col + place, N)), device_id_type=MESH,
        )
        return copy, own

    def q_source(slot, at):
        job = jobs[slot]
        used = jnp.logical_and(job >= 0, among(REACH, lax.rem(job + REACH[at], N)))
        source = lax.rem(row - REACH[at] + N, N)
        own = mine == 0 if REACH[at] == 0 else jnp.bool_(False)
        return used, own, source

    def c_copy(slot, at):
        coarse = lax.rem(row + jobs[slot] + N, N)
        target = lax.rem(row + REACH[at], N)
        own = jnp.logical_and(coarse == row, target == col)
        copy = pltpu.make_async_remote_copy(
            src_ref=c_send.at[slot, at], dst_ref=c_recv.at[at],
            send_sem=c_send_sem.at[slot, at], recv_sem=c_recv_sem.at[at],
            device_id=(coarse, target), device_id_type=MESH,
        )
        return copy, own

    def c_source(at):
        fine = lax.rem(col - REACH[at] + N, N)
        offset = lax.rem(row - fine + N, N)
        used = among(tuple(PLACE[0]), offset)
        place, slot = place_of(fine, offset)
        place = lax.rem(fine + place, N)
        own = jnp.logical_and(fine == row, place == col)
        return used, own, (fine, place), slot

    both = jnp.logical_and
    barrier = pltpu.get_barrier_semaphore()
    awaited = jnp.int32(0)
    for at in range(len(REACH)):
        used, own, source, _ = c_source(at)

        @pl.when(both(used, ~own))
        def _():
            pl.semaphore_signal(barrier, inc=1, device_id=source, device_id_type=MESH)

        awaited += jnp.where(both(live, ~q_copy(at)[1]), 1, 0)
        for slot in range(JOBS):
            used, own, source = q_source(slot, at)

            @pl.when(both(used, ~own))
            def _():
                pl.semaphore_signal(barrier, inc=1, device_id=(source, row), device_id_type=MESH)

            awaited += jnp.where(both(jobs[slot] >= 0, ~c_copy(slot, at)[1]), 1, 0)

    load_a.wait()

    @pl.when(live)
    def _():
        def build(i, carry):
            turned = [a_ref[i, s].T for s in range(SLOTS)]
            cols = pl.ds(pl.multiple_of(i * B, B), B)
            for k in range(ROWS):
                tile = jnp.zeros((B, B), jnp.float32)
                for s in range(SLOTS):
                    hit = jnp.logical_and(a_cols[s, i] == col * ROWS + k, s < a_count[0, i])
                    tile += jnp.where(hit, 1.0, 0.0) * turned[s]
                high, low = split(tile)
                a_high[k * B:(k + 1) * B, cols] = high
                a_low[k * B:(k + 1) * B, cols] = low
            return carry

        lax.fori_loop(0, ROWS, build, 0)

    load_p.wait()

    def merge(step, carry):
        i, part = step // PARTS, step % PARTS
        rows = pl.ds(pl.multiple_of(part * (B // PARTS), B // PARTS), B // PARTS)
        into = pl.ds(pl.multiple_of(step * (B // PARTS), B // PARTS), B // PARTS)
        tiles = [p_ref[i, t, rows, :] for t in range(8)]
        for at in range(len(REACH)):
            if REACH[at] == 8:
                tile = tiles[1]
            else:
                tile = tiles[0] if REACH[at] == 0 else None
                for t in range(2, 8):
                    hit = p_cols[t, row * ROWS + i] == lax.rem(row + REACH[at], N)
                    term = jnp.where(hit, 1.0, 0.0) * tiles[t]
                    tile = term if tile is None else tile + term
            high, low = split(tile)
            p_high[into, at * B:(at + 1) * B] = high
            p_low[into, at * B:(at + 1) * B] = low
        return carry

    lax.fori_loop(0, ROWS * PARTS, merge, 0)

    for pair in range(len(REACH) // 2):
        @pl.when(live)
        def _():
            cols = slice(pair * 2 * B, (pair + 1) * 2 * B)

            def chunk(n, carry):
                rows = pl.ds(pl.multiple_of(n * CHUNK, CHUNK), CHUNK)
                both_units = dot3(a_high[rows, :], a_low[rows, :], p_high[:, cols], p_low[:, cols])
                q_send[2 * pair, rows, :] = both_units[:, :B]
                q_send[2 * pair + 1, rows, :] = both_units[:, B:]
                return carry

            lax.fori_loop(0, K // CHUNK, chunk, 0)

        if pair == 0:
            @pl.when(awaited > 0)
            def _():
                pl.semaphore_wait(barrier, awaited)

        for at in (2 * pair, 2 * pair + 1):
            copy, own = q_copy(at)

            @pl.when(both(live, ~own))
            def _():
                copy.start()

    for slot in range(JOBS):
        @pl.when(jobs[slot] >= 0)
        def _():
            total[...] = jnp.zeros_like(total)
            for at in range(len(REACH)):
                used, own, _ = q_source(slot, at)

                @pl.when(both(used, ~own))
                def _():
                    pltpu.make_async_remote_copy(
                        src_ref=q_send.at[at], dst_ref=q_recv.at[slot, at],
                        send_sem=q_send_sem.at[at], recv_sem=q_recv_sem.at[slot, at],
                        device_id=(row, col), device_id_type=MESH,
                    ).wait_recv()
                    total[...] += q_recv[slot, at]

                @pl.when(both(used, own))
                def _():
                    total[...] += q_send[pick(REACH_AT, jobs[slot])]

            for k in range(ROWS):
                high, low = split(total[k * B:(k + 1) * B, :].T)
                sums[:B, k * B:(k + 1) * B] = high
                sums[B:, k * B:(k + 1) * B] = low
            for n in range(3):
                cols = slice(n * 2 * B, (n + 1) * 2 * B)
                tiles = jnp.dot(sums[...], p_high[:, cols], preferred_element_type=jnp.float32)
                tiles = tiles[:B] + tiles[B:] + jnp.dot(sums[:B, :], p_low[:, cols], preferred_element_type=jnp.float32)
                for half in range(2):
                    at = 2 * n + half
                    c_send[slot, at] = tiles[:, half * B:(half + 1) * B]
                    copy, own = c_copy(slot, at)

                    @pl.when(~own)
                    def _():
                        copy.start()

    out[...] = jnp.zeros_like(out)
    for at in range(len(REACH)):
        used, own, _, slot = c_source(at)

        @pl.when(both(used, ~own))
        def _():
            pltpu.make_async_remote_copy(
                src_ref=c_send.at[0, at], dst_ref=c_recv.at[at],
                send_sem=c_send_sem.at[0, at], recv_sem=c_recv_sem.at[at],
                device_id=(row, col), device_id_type=MESH,
            ).wait_recv()
            out[0, 0] += c_recv[at]

        @pl.when(both(used, own))
        def _():
            out[0, 0] += c_send[slot, at]

    for at in range(len(REACH)):
        copy, own = q_copy(at)

        @pl.when(both(live, ~own))
        def _():
            copy.wait_send()

        for slot in range(JOBS):
            copy, own = c_copy(slot, at)

            @pl.when(both(jobs[slot] >= 0, ~own))
            def _():
                copy.wait_send()


def on_device(a_vals, a_cols, a_count, p_vals, p_cols):
    smem = pl.BlockSpec(memory_space=pltpu.SMEM)
    hbm = pl.BlockSpec(memory_space=pl.ANY)
    spots = len(REACH)
    return pl.pallas_call(
        kernel,
        out_shape=jax.ShapeDtypeStruct((1, 1, B, B), jnp.float32),
        in_specs=[smem, smem, smem, hbm, hbm],
        out_specs=pl.BlockSpec(memory_space=pltpu.VMEM),
        scratch_shapes=[
            pltpu.VMEM((ROWS, SLOTS, B, B), jnp.float32),
            pltpu.VMEM((ROWS, 8, B, B), jnp.float32),
            pltpu.VMEM((K, K), jnp.bfloat16),
            pltpu.VMEM((K, K), jnp.bfloat16),
            pltpu.VMEM((K, spots * B), jnp.bfloat16),
            pltpu.VMEM((K, spots * B), jnp.bfloat16),
            pltpu.VMEM((2 * B, K), jnp.bfloat16),
            pltpu.VMEM((spots, K, B), jnp.float32),
            pltpu.VMEM((JOBS, spots, K, B), jnp.float32),
            pltpu.VMEM((JOBS, spots, B, B), jnp.float32),
            pltpu.VMEM((spots, B, B), jnp.float32),
            pltpu.VMEM((K, B), jnp.float32),
            pltpu.SemaphoreType.DMA((2,)),
            pltpu.SemaphoreType.DMA((spots,)),
            pltpu.SemaphoreType.DMA((JOBS, spots)),
            pltpu.SemaphoreType.DMA((JOBS, spots)),
            pltpu.SemaphoreType.DMA((spots,)),
        ],
        compiler_params=pltpu.CompilerParams(
            collective_id=0, has_side_effects=True, vmem_limit_bytes=60 << 20
        ),
    )(a_cols.T, a_count.T, p_cols.T, a_vals, p_vals)


def solution(mesh):
    return jax.shard_map(
        on_device,
        mesh=mesh,
        in_specs=(
            P("row", "col", None, None),
            P("row", "col"),
            P("row", "col"),
            P("row", None, None, None),
            P(),
        ),
        out_specs=P("row", "col", None, None),
        check_vma=False,
    )
```

```python
import jax
import jax.numpy as jnp
from jax import lax
from jax.experimental import pallas as pl
from jax.experimental.pallas import tpu as pltpu
from jax.sharding import PartitionSpec as P

MESH = pl.DeviceIdType.MESH
N = 16
REACH = (8, 2, 14, 1, 15, 0)
PLACE = (
    {0: 5, 1: 57, 2: 0, 3: 60, 4: 44, 6: 28, 7: 61, 8: 12, 9: 36, 10: 4, 12: 24, 13: 8, 14: 56, 15: 1},
    {0: 61, 1: 1, 2: 4, 3: 56, 4: 36, 6: 60, 7: 57, 8: 8, 9: 20, 10: 40, 12: 28, 13: 9, 14: 0, 15: 5},
)
JOBS = 2
ORDER = (
    {0: 180944, 1: 181896, 2: 181896, 8: 181896, 14: 181896, 15: 181896},
    {0: 177416, 1: 181896, 2: 181896, 8: 181896, 14: 181896, 15: 181896},
)
ROWS = 8
SLOTS = 4
B = 128
K = ROWS * B
PARTS = 4
PARTS_SENT = 2
PART = K // PARTS_SENT


def pick(table, index):
    total = jnp.int32(0)
    for key, value in table.items():
        total = jnp.where(index == key, jnp.int32(value), total)
    return total


def among(keys, index):
    hit = index == keys[0]
    for key in keys[1:]:
        hit = jnp.logical_or(hit, index == key)
    return hit


def split(x):
    high = x.astype(jnp.bfloat16)
    return high, (x - high.astype(jnp.float32)).astype(jnp.bfloat16)


def dot3(left_high, left_low, right_high, right_low):
    total = jnp.dot(left_high, right_high, preferred_element_type=jnp.float32)
    total += jnp.dot(left_high, right_low, preferred_element_type=jnp.float32)
    return total + jnp.dot(left_low, right_high, preferred_element_type=jnp.float32)


REACH_AT = {offset: at for at, offset in enumerate(REACH)}
RELAY = len(REACH)


def place_of(fine, offset):
    code = jnp.where(fine % 2 == 0, pick(PLACE[0], offset), pick(PLACE[1], offset))
    return code // 4, code % 4


def job_of(fine, place, slot):
    tables = [{code // 4: job + 1 for job, code in table.items() if code % 4 == slot} for table in PLACE]
    return jnp.where(fine % 2 == 0, pick(tables[0], place), pick(tables[1], place)) - 1


def detour(row):
    low, even = row % 4 < 2, row // 4 % 2 == 0
    return low == even, jnp.where(low, N - 4, 4)


def kernel(
    a_cols, a_count, p_cols, a_hbm, p_hbm, out,
    a_ref, p_ref, a_high, a_low, p_high, p_low, sums,
    q_send, q_recv, c_send, c_recv, total,
    load_sem, q_send_sem, q_recv_sem, relay_sem, c_send_sem, c_recv_sem,
):
    row, col = lax.axis_index("row"), lax.axis_index("col")
    mine = lax.rem(col - row + N, N)
    live = among(REACH, mine)
    jobs = [job_of(row, mine, slot) for slot in range(JOBS)]

    load_a = pltpu.make_async_copy(a_hbm, a_ref, load_sem.at[0])
    load_p = pltpu.make_async_copy(p_hbm, p_ref, load_sem.at[1])
    load_a.start()
    load_p.start()

    sequence = jnp.where(col % 2 == 0, pick(ORDER[0], mine), pick(ORDER[1], mine))
    turns = [sequence // 8**turn % 8 for turn in range(len(REACH))]

    def q_copy(at, part):
        offset = lax.rem(pick(dict(enumerate(REACH)), at) - mine + N, N)
        place, slot = place_of(col, offset)
        spot = pick(REACH_AT, mine)
        own = jnp.logical_and(mine == 0, place == 0)
        around, step = detour(row)
        around = jnp.logical_and(around, mine == 8)
        spot = jnp.where(around, RELAY, spot)
        target = jnp.where(around, lax.rem(row + step, N), col)
        copy = pltpu.make_async_remote_copy(
            src_ref=q_send.at[at, part], dst_ref=q_recv.at[slot, spot, part],
            send_sem=q_send_sem.at[at, part], recv_sem=q_recv_sem.at[slot, spot, part],
            device_id=(target, lax.rem(col + place, N)), device_id_type=MESH,
        )
        return copy, own

    around, step = detour(lax.rem(row + 4, N))
    relays = jnp.where(row % 4 < 2, around, detour(lax.rem(row + 12, N))[0])
    onward = lax.rem(row + step, N)
    relayed = [job_of(onward, lax.rem(col - onward + N, N), slot) for slot in range(JOBS)]
    relayed = [
        jnp.logical_and(relays, jnp.logical_and(job >= 0, among(REACH, lax.rem(job + 8, N)))) for job in relayed
    ]

    def relay_copy(slot, part):
        return pltpu.make_async_remote_copy(
            src_ref=q_recv.at[slot, RELAY, part], dst_ref=q_recv.at[slot, REACH_AT[8], part],
            send_sem=relay_sem.at[slot, part], recv_sem=q_recv_sem.at[slot, REACH_AT[8], part],
            device_id=(onward, col), device_id_type=MESH,
        )

    def q_source(slot, at):
        job = jobs[slot]
        used = jnp.logical_and(job >= 0, among(REACH, lax.rem(job + REACH[at], N)))
        fine = lax.rem(row - REACH[at] + N, N)
        source = fine, row
        if REACH[at] == 8:
            around, step = detour(fine)
            source = jnp.where(around, lax.rem(fine + step, N), fine), jnp.where(around, col, row)
        own = mine == 0 if REACH[at] == 0 else jnp.bool_(False)
        return used, own, source

    def c_copy(slot, at):
        coarse = lax.rem(row + jobs[slot] + N, N)
        target = lax.rem(row + REACH[at], N)
        own = jnp.logical_and(coarse == row, target == col)
        copy = pltpu.make_async_remote_copy(
            src_ref=c_send.at[slot, at], dst_ref=c_recv.at[at],
            send_sem=c_send_sem.at[slot, at], recv_sem=c_recv_sem.at[at],
            device_id=(coarse, target), device_id_type=MESH,
        )
        return copy, own

    def c_source(at):
        fine = lax.rem(col - REACH[at] + N, N)
        offset = lax.rem(row - fine + N, N)
        used = among(tuple(PLACE[0]), offset)
        place, slot = place_of(fine, offset)
        place = lax.rem(fine + place, N)
        own = jnp.logical_and(fine == row, place == col)
        return used, own, (fine, place), slot

    both = jnp.logical_and
    barrier = pltpu.get_barrier_semaphore()
    awaited = jnp.int32(0)
    for at in range(len(REACH)):
        used, own, source, _ = c_source(at)

        @pl.when(both(used, ~own))
        def _():
            pl.semaphore_signal(barrier, inc=1, device_id=source, device_id_type=MESH)

        awaited += jnp.where(both(live, ~q_copy(at, 0)[1]), 1, 0)
        for slot in range(JOBS):
            used, own, source = q_source(slot, at)

            @pl.when(both(used, ~own))
            def _():
                pl.semaphore_signal(barrier, inc=1, device_id=source, device_id_type=MESH)

            awaited += jnp.where(both(jobs[slot] >= 0, ~c_copy(slot, at)[1]), 1, 0)

    origin = lax.rem(onward + 8, N)
    for slot in range(JOBS):
        @pl.when(relayed[slot])
        def _():
            pl.semaphore_signal(barrier, inc=1, device_id=(origin, onward), device_id_type=MESH)

        awaited += jnp.where(relayed[slot], 1, 0)

    load_a.wait()

    @pl.when(live)
    def _():
        def build(i, carry):
            turned = [a_ref[i, s].T for s in range(SLOTS)]
            cols = pl.ds(pl.multiple_of(i * B, B), B)
            for k in range(ROWS):
                tile = jnp.zeros((B, B), jnp.float32)
                for s in range(SLOTS):
                    hit = jnp.logical_and(a_cols[s, i] == col * ROWS + k, s < a_count[0, i])
                    tile += jnp.where(hit, 1.0, 0.0) * turned[s]
                high, low = split(tile)
                a_high[k * B:(k + 1) * B, cols] = high
                a_low[k * B:(k + 1) * B, cols] = low
            return carry

        lax.fori_loop(0, ROWS, build, 0)

    load_p.wait()

    def merge(step, carry):
        i, part = step // PARTS, step % PARTS
        rows = pl.ds(pl.multiple_of(part * (B // PARTS), B // PARTS), B // PARTS)
        into = pl.ds(pl.multiple_of(step * (B // PARTS), B // PARTS), B // PARTS)
        tiles = [p_ref[i, t, rows, :] for t in range(8)]
        for at in range(len(REACH)):
            if REACH[at] == 8:
                tile = tiles[1]
            else:
                tile = tiles[0] if REACH[at] == 0 else None
                for t in range(2, 8):
                    hit = p_cols[t, row * ROWS + i] == lax.rem(row + REACH[at], N)
                    term = jnp.where(hit, 1.0, 0.0) * tiles[t]
                    tile = term if tile is None else tile + term
            high, low = split(tile)
            p_high[at, into] = high
            p_low[at, into] = low
        return carry

    lax.fori_loop(0, ROWS * PARTS, merge, 0)

    def two(ref, first, second, rows=slice(None)):
        return jnp.concatenate([ref[first, rows], ref[second, rows]], axis=1)

    for part in range(PARTS_SENT):
        for pair in range(len(REACH) // 2):
            units = turns[2 * pair:2 * pair + 2]

            @pl.when(live)
            def _():
                rows = slice(part * PART, (part + 1) * PART)
                products = dot3(a_high[rows, :], a_low[rows, :], two(p_high, *units), two(p_low, *units))
                q_send[units[0], part] = products[:, :B]
                q_send[units[1], part] = products[:, B:]

            if pair == 0 and part == 0:
                @pl.when(awaited > 0)
                def _():
                    pl.semaphore_wait(barrier, awaited)

            for at in units:
                copy, own = q_copy(at, part)

                @pl.when(both(live, ~own))
                def _():
                    copy.start()

    for slot in range(JOBS):
        for part in range(PARTS_SENT):
            @pl.when(relayed[slot])
            def _():
                pltpu.make_async_remote_copy(
                    src_ref=q_send.at[0, part], dst_ref=q_recv.at[slot, RELAY, part],
                    send_sem=q_send_sem.at[0, part], recv_sem=q_recv_sem.at[slot, RELAY, part],
                    device_id=(row, col), device_id_type=MESH,
                ).wait_recv()
                relay_copy(slot, part).start()

    for slot in range(JOBS):
        for part in range(PARTS_SENT):
            @pl.when(jobs[slot] >= 0)
            def _():
                total[...] = jnp.zeros_like(total)
                for at in range(len(REACH)):
                    used, own, _ = q_source(slot, at)

                    @pl.when(both(used, ~own))
                    def _():
                        pltpu.make_async_remote_copy(
                            src_ref=q_send.at[at, part], dst_ref=q_recv.at[slot, at, part],
                            send_sem=q_send_sem.at[at, part], recv_sem=q_recv_sem.at[slot, at, part],
                            device_id=(row, col), device_id_type=MESH,
                        ).wait_recv()
                        total[...] += q_recv[slot, at, part]

                    @pl.when(both(used, own))
                    def _():
                        total[...] += q_send[pick(REACH_AT, jobs[slot]), part]

                for k in range(PART // B):
                    high, low = split(total[k * B:(k + 1) * B, :].T)
                    sums[:B, k * B:(k + 1) * B] = high
                    sums[B:, k * B:(k + 1) * B] = low
                rows = slice(part * PART, (part + 1) * PART)
                for n in range(3):
                    tiles = jnp.dot(sums[...], two(p_high, 2 * n, 2 * n + 1, rows), preferred_element_type=jnp.float32)
                    tiles = tiles[:B] + tiles[B:] + jnp.dot(
                        sums[:B, :], two(p_low, 2 * n, 2 * n + 1, rows), preferred_element_type=jnp.float32
                    )
                    for half in range(2):
                        at = 2 * n + half
                        tile = tiles[:, half * B:(half + 1) * B]
                        c_send[slot, at] = tile if part == 0 else c_send[slot, at] + tile
                        if part == PARTS_SENT - 1:
                            copy, own = c_copy(slot, at)

                            @pl.when(~own)
                            def _():
                                copy.start()

    out[...] = jnp.zeros_like(out)
    for at in range(len(REACH)):
        used, own, _, slot = c_source(at)

        @pl.when(both(used, ~own))
        def _():
            pltpu.make_async_remote_copy(
                src_ref=c_send.at[0, at], dst_ref=c_recv.at[at],
                send_sem=c_send_sem.at[0, at], recv_sem=c_recv_sem.at[at],
                device_id=(row, col), device_id_type=MESH,
            ).wait_recv()
            out[0, 0] += c_recv[at]

        @pl.when(both(used, own))
        def _():
            out[0, 0] += c_send[slot, at]

    for slot in range(JOBS):
        for part in range(PARTS_SENT):
            @pl.when(relayed[slot])
            def _():
                relay_copy(slot, part).wait_send()

    for at in range(len(REACH)):
        for part in range(PARTS_SENT):
            copy, own = q_copy(at, part)

            @pl.when(both(live, ~own))
            def _():
                copy.wait_send()

    for at in range(len(REACH)):
        for slot in range(JOBS):
            copy, own = c_copy(slot, at)

            @pl.when(both(jobs[slot] >= 0, ~own))
            def _():
                copy.wait_send()


def on_device(a_vals, a_cols, a_count, p_vals, p_cols):
    smem = pl.BlockSpec(memory_space=pltpu.SMEM)
    hbm = pl.BlockSpec(memory_space=pl.ANY)
    spots = len(REACH)
    return pl.pallas_call(
        kernel,
        out_shape=jax.ShapeDtypeStruct((1, 1, B, B), jnp.float32),
        in_specs=[smem, smem, smem, hbm, hbm],
        out_specs=pl.BlockSpec(memory_space=pltpu.VMEM),
        scratch_shapes=[
            pltpu.VMEM((ROWS, SLOTS, B, B), jnp.float32),
            pltpu.VMEM((ROWS, 8, B, B), jnp.float32),
            pltpu.VMEM((K, K), jnp.bfloat16),
            pltpu.VMEM((K, K), jnp.bfloat16),
            pltpu.VMEM((spots, K, B), jnp.bfloat16),
            pltpu.VMEM((spots, K, B), jnp.bfloat16),
            pltpu.VMEM((2 * B, PART), jnp.bfloat16),
            pltpu.VMEM((spots, PARTS_SENT, PART, B), jnp.float32),
            pltpu.VMEM((JOBS, spots + 1, PARTS_SENT, PART, B), jnp.float32),
            pltpu.VMEM((JOBS, spots, B, B), jnp.float32),
            pltpu.VMEM((spots, B, B), jnp.float32),
            pltpu.VMEM((PART, B), jnp.float32),
            pltpu.SemaphoreType.DMA((2,)),
            pltpu.SemaphoreType.DMA((spots, PARTS_SENT)),
            pltpu.SemaphoreType.DMA((JOBS, spots + 1, PARTS_SENT)),
            pltpu.SemaphoreType.DMA((JOBS, PARTS_SENT)),
            pltpu.SemaphoreType.DMA((JOBS, spots)),
            pltpu.SemaphoreType.DMA((spots,)),
        ],
        compiler_params=pltpu.CompilerParams(
            collective_id=0, has_side_effects=True, vmem_limit_bytes=60 << 20
        ),
    )(a_cols.T, a_count.T, p_cols.T, a_vals, p_vals)


def solution(mesh):
    return jax.shard_map(
        on_device,
        mesh=mesh,
        in_specs=(
            P("row", "col", None, None),
            P("row", "col"),
            P("row", "col"),
            P("row", None, None, None),
            P(),
        ),
        out_specs=P("row", "col", None, None),
        check_vma=False,
    )
```

```python
import jax
import jax.numpy as jnp
from jax import lax
from jax.experimental import pallas as pl
from jax.experimental.pallas import tpu as pltpu
from jax.sharding import PartitionSpec as P

MESH = pl.DeviceIdType.MESH
N = 16
REACH = (8, 14, 2, 15, 1, 0)
PLACE = (
    {0: 5, 1: 57, 2: 0, 3: 60, 4: 44, 6: 28, 7: 61, 8: 12, 9: 36, 10: 4, 12: 24, 13: 8, 14: 56, 15: 1},
    {0: 61, 1: 1, 2: 4, 3: 56, 4: 36, 6: 60, 7: 57, 8: 8, 9: 20, 10: 40, 12: 28, 13: 9, 14: 0, 15: 5},
)
JOBS = 2
ORDER = (
    {0: 180944, 1: 181896, 2: 181896, 8: 181896, 14: 181896, 15: 181896},
    {0: 177416, 1: 181896, 2: 181896, 8: 181896, 14: 181896, 15: 181896},
)
ROWS = 8
SLOTS = 4
B = 128
K = ROWS * B
PARTS = 4
PARTS_SENT = 2
PART = K // PARTS_SENT


def pick(table, index):
    total = jnp.int32(0)
    for key, value in table.items():
        total = jnp.where(index == key, jnp.int32(value), total)
    return total


def among(keys, index):
    hit = index == keys[0]
    for key in keys[1:]:
        hit = jnp.logical_or(hit, index == key)
    return hit


def split(x):
    high = x.astype(jnp.bfloat16)
    return high, (x - high.astype(jnp.float32)).astype(jnp.bfloat16)


def dot3(left_high, left_low, right_high, right_low):
    total = jnp.dot(left_high, right_high, preferred_element_type=jnp.float32)
    total += jnp.dot(left_high, right_low, preferred_element_type=jnp.float32)
    return total + jnp.dot(left_low, right_high, preferred_element_type=jnp.float32)


REACH_AT = {offset: at for at, offset in enumerate(REACH)}
RELAY = len(REACH)


def place_of(fine, offset):
    code = jnp.where(fine % 2 == 0, pick(PLACE[0], offset), pick(PLACE[1], offset))
    return code // 4, code % 4


def job_of(fine, place, slot):
    tables = [{code // 4: job + 1 for job, code in table.items() if code % 4 == slot} for table in PLACE]
    return jnp.where(fine % 2 == 0, pick(tables[0], place), pick(tables[1], place)) - 1


def detour(row):
    low, even = row % 4 < 2, row // 4 % 2 == 0
    return low == even, jnp.where(low, N - 4, 4)


def kernel(
    a_cols, a_count, p_cols, a_hbm, p_hbm, out,
    a_ref, p_ref, a_high, a_low, p_high, p_low, sums,
    q_send, q_recv, c_send, c_recv, total,
    load_sem, q_send_sem, q_recv_sem, relay_sem, c_send_sem, c_recv_sem,
):
    row, col = lax.axis_index("row"), lax.axis_index("col")
    mine = lax.rem(col - row + N, N)
    live = among(REACH, mine)
    jobs = [job_of(row, mine, slot) for slot in range(JOBS)]

    load_a = pltpu.make_async_copy(a_hbm, a_ref, load_sem.at[0])
    load_p = pltpu.make_async_copy(p_hbm, p_ref, load_sem.at[1])
    load_a.start()
    load_p.start()

    sequence = jnp.where(col % 2 == 0, pick(ORDER[0], mine), pick(ORDER[1], mine))
    turns = [sequence // 8**turn % 8 for turn in range(len(REACH))]

    def q_copy(at, part):
        offset = lax.rem(pick(dict(enumerate(REACH)), at) - mine + N, N)
        place, slot = place_of(col, offset)
        spot = pick(REACH_AT, mine)
        own = jnp.logical_and(mine == 0, place == 0)
        around, step = detour(row)
        around = jnp.logical_and(around, mine == 8)
        spot = jnp.where(around, RELAY, spot)
        target = jnp.where(around, lax.rem(row + step, N), col)
        copy = pltpu.make_async_remote_copy(
            src_ref=q_send.at[at, part], dst_ref=q_recv.at[slot, spot, part],
            send_sem=q_send_sem.at[at, part], recv_sem=q_recv_sem.at[slot, spot, part],
            device_id=(target, lax.rem(col + place, N)), device_id_type=MESH,
        )
        return copy, own

    around, step = detour(lax.rem(row + 4, N))
    relays = jnp.where(row % 4 < 2, around, detour(lax.rem(row + 12, N))[0])
    onward = lax.rem(row + step, N)
    relayed = [job_of(onward, lax.rem(col - onward + N, N), slot) for slot in range(JOBS)]
    relayed = [
        jnp.logical_and(relays, jnp.logical_and(job >= 0, among(REACH, lax.rem(job + 8, N)))) for job in relayed
    ]

    def relay_copy(slot, part):
        return pltpu.make_async_remote_copy(
            src_ref=q_recv.at[slot, RELAY, part], dst_ref=q_recv.at[slot, REACH_AT[8], part],
            send_sem=relay_sem.at[slot, part], recv_sem=q_recv_sem.at[slot, REACH_AT[8], part],
            device_id=(onward, col), device_id_type=MESH,
        )

    def q_source(slot, at):
        job = jobs[slot]
        used = jnp.logical_and(job >= 0, among(REACH, lax.rem(job + REACH[at], N)))
        fine = lax.rem(row - REACH[at] + N, N)
        source = fine, row
        if REACH[at] == 8:
            around, step = detour(fine)
            source = jnp.where(around, lax.rem(fine + step, N), fine), jnp.where(around, col, row)
        own = mine == 0 if REACH[at] == 0 else jnp.bool_(False)
        return used, own, source

    def c_copy(slot, at):
        coarse = lax.rem(row + jobs[slot] + N, N)
        target = lax.rem(row + REACH[at], N)
        own = jnp.logical_and(coarse == row, target == col)
        copy = pltpu.make_async_remote_copy(
            src_ref=c_send.at[slot, at], dst_ref=c_recv.at[at],
            send_sem=c_send_sem.at[slot, at], recv_sem=c_recv_sem.at[at],
            device_id=(coarse, target), device_id_type=MESH,
        )
        return copy, own

    def c_source(at):
        fine = lax.rem(col - REACH[at] + N, N)
        offset = lax.rem(row - fine + N, N)
        used = among(tuple(PLACE[0]), offset)
        place, slot = place_of(fine, offset)
        place = lax.rem(fine + place, N)
        own = jnp.logical_and(fine == row, place == col)
        return used, own, (fine, place), slot

    both = jnp.logical_and
    barrier = pltpu.get_barrier_semaphore()
    awaited = jnp.int32(0)
    for at in range(len(REACH)):
        used, own, source, _ = c_source(at)

        @pl.when(both(used, ~own))
        def _():
            pl.semaphore_signal(barrier, inc=1, device_id=source, device_id_type=MESH)

        awaited += jnp.where(both(live, ~q_copy(at, 0)[1]), 1, 0)
        for slot in range(JOBS):
            used, own, source = q_source(slot, at)

            @pl.when(both(used, ~own))
            def _():
                pl.semaphore_signal(barrier, inc=1, device_id=source, device_id_type=MESH)

            awaited += jnp.where(both(jobs[slot] >= 0, ~c_copy(slot, at)[1]), 1, 0)

    origin = lax.rem(onward + 8, N)
    for slot in range(JOBS):
        @pl.when(relayed[slot])
        def _():
            pl.semaphore_signal(barrier, inc=1, device_id=(origin, onward), device_id_type=MESH)

        awaited += jnp.where(relayed[slot], 1, 0)

    load_a.wait()

    @pl.when(live)
    def _():
        def build(i, carry):
            turned = [a_ref[i, s].T for s in range(SLOTS)]
            cols = pl.ds(pl.multiple_of(i * B, B), B)
            for k in range(ROWS):
                tile = jnp.zeros((B, B), jnp.float32)
                for s in range(SLOTS):
                    hit = jnp.logical_and(a_cols[s, i] == col * ROWS + k, s < a_count[0, i])
                    tile += jnp.where(hit, 1.0, 0.0) * turned[s]
                high, low = split(tile)
                a_high[k * B:(k + 1) * B, cols] = high
                a_low[k * B:(k + 1) * B, cols] = low
            return carry

        lax.fori_loop(0, ROWS, build, 0)

    load_p.wait()

    def merge(step, carry):
        i, part = step // PARTS, step % PARTS
        rows = pl.ds(pl.multiple_of(part * (B // PARTS), B // PARTS), B // PARTS)
        into = pl.ds(pl.multiple_of(step * (B // PARTS), B // PARTS), B // PARTS)
        tiles = [p_ref[i, t, rows, :] for t in range(8)]
        for at in range(len(REACH)):
            if REACH[at] == 8:
                tile = tiles[1]
            else:
                tile = tiles[0] if REACH[at] == 0 else None
                for t in range(2, 8):
                    hit = p_cols[t, row * ROWS + i] == lax.rem(row + REACH[at], N)
                    term = jnp.where(hit, 1.0, 0.0) * tiles[t]
                    tile = term if tile is None else tile + term
            high, low = split(tile)
            p_high[at, into] = high
            p_low[at, into] = low
        return carry

    lax.fori_loop(0, ROWS * PARTS, merge, 0)

    def two(ref, first, second, rows=slice(None)):
        return jnp.concatenate([ref[first, rows], ref[second, rows]], axis=1)

    for part in range(PARTS_SENT):
        for pair in range(len(REACH) // 2):
            units = turns[2 * pair:2 * pair + 2]

            @pl.when(live)
            def _():
                rows = slice(part * PART, (part + 1) * PART)
                products = dot3(a_high[rows, :], a_low[rows, :], two(p_high, *units), two(p_low, *units))
                q_send[units[0], part] = products[:, :B]
                q_send[units[1], part] = products[:, B:]

            if part == 0 and pair == 0:
                continue
            if part == 0 and pair == 1:
                units = turns[:4]

                @pl.when(awaited > 0)
                def _():
                    pl.semaphore_wait(barrier, awaited)

            for at in units:
                copy, own = q_copy(at, part)

                @pl.when(both(live, ~own))
                def _():
                    copy.start()

    for slot in range(JOBS):
        for part in range(PARTS_SENT):
            @pl.when(relayed[slot])
            def _():
                pltpu.make_async_remote_copy(
                    src_ref=q_send.at[0, part], dst_ref=q_recv.at[slot, RELAY, part],
                    send_sem=q_send_sem.at[0, part], recv_sem=q_recv_sem.at[slot, RELAY, part],
                    device_id=(row, col), device_id_type=MESH,
                ).wait_recv()
                relay_copy(slot, part).start()

    for part in range(PARTS_SENT):
        for slot in range(JOBS):
            @pl.when(jobs[slot] >= 0)
            def _():
                total[...] = jnp.zeros_like(total)
                for at in range(len(REACH)):
                    used, own, _ = q_source(slot, at)

                    @pl.when(both(used, ~own))
                    def _():
                        pltpu.make_async_remote_copy(
                            src_ref=q_send.at[at, part], dst_ref=q_recv.at[slot, at, part],
                            send_sem=q_send_sem.at[at, part], recv_sem=q_recv_sem.at[slot, at, part],
                            device_id=(row, col), device_id_type=MESH,
                        ).wait_recv()
                        total[...] += q_recv[slot, at, part]

                    @pl.when(both(used, own))
                    def _():
                        total[...] += q_send[pick(REACH_AT, jobs[slot]), part]

                for k in range(PART // B):
                    high, low = split(total[k * B:(k + 1) * B, :].T)
                    sums[:B, k * B:(k + 1) * B] = high
                    sums[B:, k * B:(k + 1) * B] = low
                rows = slice(part * PART, (part + 1) * PART)
                for n in range(3):
                    tiles = jnp.dot(sums[...], two(p_high, 2 * n, 2 * n + 1, rows), preferred_element_type=jnp.float32)
                    tiles = tiles[:B] + tiles[B:] + jnp.dot(
                        sums[:B, :], two(p_low, 2 * n, 2 * n + 1, rows), preferred_element_type=jnp.float32
                    )
                    for half in range(2):
                        at = 2 * n + half
                        tile = tiles[:, half * B:(half + 1) * B]
                        c_send[slot, at] = tile if part == 0 else c_send[slot, at] + tile
                        if part == PARTS_SENT - 1:
                            copy, own = c_copy(slot, at)

                            @pl.when(~own)
                            def _():
                                copy.start()

    out[...] = jnp.zeros_like(out)
    for at in range(len(REACH)):
        used, own, _, slot = c_source(at)

        @pl.when(both(used, ~own))
        def _():
            pltpu.make_async_remote_copy(
                src_ref=c_send.at[0, at], dst_ref=c_recv.at[at],
                send_sem=c_send_sem.at[0, at], recv_sem=c_recv_sem.at[at],
                device_id=(row, col), device_id_type=MESH,
            ).wait_recv()
            out[0, 0] += c_recv[at]

        @pl.when(both(used, own))
        def _():
            out[0, 0] += c_send[slot, at]

    for slot in range(JOBS):
        for part in range(PARTS_SENT):
            @pl.when(relayed[slot])
            def _():
                relay_copy(slot, part).wait_send()

    for at in range(len(REACH)):
        for part in range(PARTS_SENT):
            copy, own = q_copy(at, part)

            @pl.when(both(live, ~own))
            def _():
                copy.wait_send()

    for at in range(len(REACH)):
        for slot in range(JOBS):
            copy, own = c_copy(slot, at)

            @pl.when(both(jobs[slot] >= 0, ~own))
            def _():
                copy.wait_send()


def on_device(a_vals, a_cols, a_count, p_vals, p_cols):
    smem = pl.BlockSpec(memory_space=pltpu.SMEM)
    hbm = pl.BlockSpec(memory_space=pl.ANY)
    spots = len(REACH)
    return pl.pallas_call(
        kernel,
        out_shape=jax.ShapeDtypeStruct((1, 1, B, B), jnp.float32),
        in_specs=[smem, smem, smem, hbm, hbm],
        out_specs=pl.BlockSpec(memory_space=pltpu.VMEM),
        scratch_shapes=[
            pltpu.VMEM((ROWS, SLOTS, B, B), jnp.float32),
            pltpu.VMEM((ROWS, 8, B, B), jnp.float32),
            pltpu.VMEM((K, K), jnp.bfloat16),
            pltpu.VMEM((K, K), jnp.bfloat16),
            pltpu.VMEM((spots, K, B), jnp.bfloat16),
            pltpu.VMEM((spots, K, B), jnp.bfloat16),
            pltpu.VMEM((2 * B, PART), jnp.bfloat16),
            pltpu.VMEM((spots, PARTS_SENT, PART, B), jnp.float32),
            pltpu.VMEM((JOBS, spots + 1, PARTS_SENT, PART, B), jnp.float32),
            pltpu.VMEM((JOBS, spots, B, B), jnp.float32),
            pltpu.VMEM((spots, B, B), jnp.float32),
            pltpu.VMEM((PART, B), jnp.float32),
            pltpu.SemaphoreType.DMA((2,)),
            pltpu.SemaphoreType.DMA((spots, PARTS_SENT)),
            pltpu.SemaphoreType.DMA((JOBS, spots + 1, PARTS_SENT)),
            pltpu.SemaphoreType.DMA((JOBS, PARTS_SENT)),
            pltpu.SemaphoreType.DMA((JOBS, spots)),
            pltpu.SemaphoreType.DMA((spots,)),
        ],
        compiler_params=pltpu.CompilerParams(
            collective_id=0, has_side_effects=True, vmem_limit_bytes=60 << 20
        ),
    )(a_cols.T, a_count.T, p_cols.T, a_vals, p_vals)


def solution(mesh):
    return jax.shard_map(
        on_device,
        mesh=mesh,
        in_specs=(
            P("row", "col", None, None),
            P("row", "col"),
            P("row", "col"),
            P("row", None, None, None),
            P(),
        ),
        out_specs=P("row", "col", None, None),
        check_vma=False,
    )
```
